32 devices in a mesh: dp: 8 (over z, x), mp: 4 (over y, core).
Axes of the slice: x: 2, y: 2, z: 4, core: 2. Of those that a mesh axis runs over, the one named last changes fastest.
Arguments:
- partials: bfloat16 [8, 8, 640, 1024], P('dp', None, None, 'mp'), may hold values from -6 to 6
- owner: int32 [8], replicated, may hold values from 0 to 7, as said below
- rowblock: int32 [8, 8], replicated, may hold values from 0 to 7, each once within a row
- factor: float32 [8, 640, 2, 640], P('dp', 'mp'), as said below
- basis: float32 [8, 640, 2, 640], P('dp', 'mp'), may hold values from -0.25 to 0.25
- moment1: float32 [8, 2, 640, 1024], P('dp', None, None, 'mp'), may hold values from -1.5 to 1.5
- moment2: float32 [8, 2, 640, 1024], P('dp', None, None, 'mp'), may hold values from 0.001 to 0.02
- master: float32 [8, 2, 640, 1024], P('dp', None, None, 'mp'), may hold values from -6 to 6
Outputs:
- train_weights: float32 [8, 8, 80, 1024], P(None, 'dp', None, 'mp')
- new_basis: float32 [8, 640, 2, 640], P('dp', 'mp')
The draws below stay inside these ranges and needn't reach their ends.
Inputs may be any that keep to these rules, and one draw needn't show every extreme that they name: `owner`: each data group owns at most 2 matrices and one owns exactly 2; the first and the last data group each own a matrix. `rowblock`: each row is a permutation of the data groups' row blocks. `factor`: symmetric in its two 640 dimensions.
All inputs are finite; a program needn't handle non-finite values.
Results may differ from the reference program's by a relative error of at most 0.0003.
Values sent between devices are 32-bit elements; how exact they have to be, the bound alone decides.
A program may use at most 128 MiB of HBM per device.

```python
import math
import jax
import jax.numpy as jnp
from jax import lax

D = 640
C = 1024
NMAT = 8
SLOTS = 2
NS_ITERS = 4
N_DP = 8


def draw_owner(key, part):
    base = jax.random.fold_in(key, 11)
    key_flip = jax.random.fold_in(base, 1)
    key_middle = jax.random.fold_in(base, 2)
    key_order = jax.random.fold_in(base, 3)
    flip = jax.random.randint(key_flip, (), 0, 2).astype(jnp.int32)
    top_group = jnp.int32(N_DP - 1)
    doubled = flip * top_group
    single = (1 - flip) * top_group
    middle = (jax.random.permutation(key_middle, N_DP - 2) + 1).astype(jnp.int32)
    chosen = jnp.concatenate([jnp.stack([doubled, doubled, single]), middle[:NMAT - 3]]).astype(jnp.int32)
    order = jax.random.permutation(key_order, NMAT)
    return jnp.zeros((NMAT,), jnp.int32).at[order].set(chosen)


def draw_factor(key, part):
    shape = (N_DP, D, SLOTS, D)
    raw = jax.random.normal(jax.random.fold_in(key, 5), shape, jnp.float32)
    symmetric = 0.5 * (raw + jnp.transpose(raw, (0, 3, 2, 1)))
    ident = (jnp.arange(D)[:, None, None] == jnp.arange(D)[None, None, :]).astype(jnp.float32)
    return 3.0 * ident[None] + symmetric * D ** (-0.5)


def strengthened(drawn, stream_key, source, target, shards_of, factor):
    owner, partner = [(jnp.arange(drawn.shape[dim]) // (drawn.shape[dim] // shards_of)).reshape([-1 if axis == dim else 1 for axis in range(drawn.ndim)]) for dim in (source, target)]
    chosen = jax.random.permutation(stream_key, shards_of)[partner]
    strong = (owner == chosen) | (owner == (partner + shards_of // 2) % shards_of)
    return jnp.where(strong, factor * drawn, drawn)


def shard_levels(rng, shape, shards, least, top_value):
    def one(dim, parts):
        heights = jax.random.uniform(jax.random.fold_in(jax.random.fold_in(rng, 6), dim), (parts,), jnp.float32, least / len(shards), top_value / len(shards))
        return jnp.repeat(jnp.exp(heights), shape[dim] // parts).reshape((-1,) + (1,) * (len(shape) - dim - 1))

    gain = one(*shards[0])
    for cut in shards[1:]:
        gain = gain * one(*cut)
    return gain


def bell_draw(rng, extent, width, reach, split=(), kind=jnp.bfloat16):
    gain = shard_levels(rng, extent, split, -0.22, 0.18) if split else 1.0
    drawn = jax.random.normal(rng, extent, jnp.float32) * width * gain
    return jnp.minimum(jnp.maximum(drawn, -reach), reach).astype(kind)


def noise_with(rng, dims, spread, reach, cuts, heavy, kind=jnp.bfloat16):
    drawn = spread * jax.random.normal(rng, dims, jnp.float32)
    if cuts:
        drawn = drawn * shard_levels(rng, dims, cuts, -0.22, 0.18)
    return jnp.clip(strengthened(drawn, jax.random.fold_in(rng, 3), *heavy), -reach, reach).astype(kind)


def setup_inputs(seed: int = 0) -> dict:
    key_list = jax.random.split(jax.random.key(seed), 9)
    partials = noise_with(key_list[0], (N_DP, NMAT, D, C), 1.0, 6.0, ((0, 8), (3, 4)), (0, 2, 8, 2.0))
    owner = draw_owner(jax.random.fold_in(key_list[8], 71), 0)
    rowblock = jax.vmap(lambda own: jax.random.permutation(own, N_DP))(jax.random.split(key_list[2], NMAT)).reshape((NMAT, N_DP)).astype(jnp.int32)
    factor = draw_factor(jax.random.fold_in(key_list[8], 71), 0)
    basis = bell_draw(key_list[4], (N_DP, D, SLOTS, D), D ** -0.5, 0.25, ((0, 8), (1, 4)), jnp.float32)
    moment1 = bell_draw(key_list[5], (N_DP, SLOTS, D, C), 0.1, 1.5, ((0, 8), (3, 4)), jnp.float32)
    moment2 = jnp.clip(jnp.exp(math.log(0.02) - 2.9957322 * jax.random.uniform(key_list[6], (N_DP, SLOTS, D, C), jnp.float32) ** shard_levels(key_list[6], (N_DP, SLOTS, D, C), ((0, 8), (3, 4)), -0.2, 0.2)), 0.001, 0.02)
    master = bell_draw(key_list[7], (N_DP, SLOTS, D, C), 1.0, 6.0, ((0, 8), (3, 4)), jnp.float32)
    return dict(partials=partials, owner=owner, rowblock=rowblock, factor=factor, basis=basis, moment1=moment1, moment2=moment2, master=master)


def slots_of(owner):
    order = jnp.arange(owner.shape[0])
    same = owner[:, None] == owner[None, :]
    earlier = order[None, :] < order[:, None]
    return lax.optimization_barrier(jnp.sum((same & earlier).astype(jnp.int32), axis=1))

def reference(partials, owner, rowblock, factor, basis, moment1, moment2, master):
    top_precision = lax.Precision.HIGHEST

    def accumulate(index, total):
        return total + partials[index].astype(jnp.float32)
    summed = lax.fori_loop(0, N_DP, accumulate, jnp.zeros((NMAT, D, C), jnp.float32))
    query_gradient = summed / N_DP
    slot = slots_of(owner)
    new_basis = jnp.zeros((N_DP, D, SLOTS, D), jnp.float32)
    trained = []
    for matrix in range(NMAT):
        group = owner[matrix]
        place = slot[matrix]
        current = basis[group, :, place, :]
        turned_gradient = jnp.dot(current.T, query_gradient[matrix], precision=top_precision)
        leading_moment = 0.9 * moment1[group, place] + 0.1 * turned_gradient
        trailing_moment = 0.95 * moment2[group, place] + 0.05 * turned_gradient * turned_gradient
        direction = jnp.dot(current, leading_moment / (jnp.sqrt(trailing_moment) + 1e-08), precision=top_precision)
        held = master[group, place]
        weights = held - 0.1 * (direction + 0.1 * held)
        blocks = weights.reshape(N_DP, D // N_DP, C)
        trained.append(jnp.take(blocks, rowblock[matrix], axis=0))
        statistic = 0.95 * factor[group, :, place, :] + 0.05 * jnp.dot(query_gradient[matrix], query_gradient[matrix].T, precision=top_precision)
        power = jnp.dot(statistic, current, precision=top_precision)
        iterate = power / jnp.sqrt(jnp.sum(power * power) + 1e-06)
        for step in range(NS_ITERS):
            inner = jnp.dot(iterate, iterate.T, precision=top_precision)
            squared = jnp.dot(inner, inner, precision=top_precision)
            merged_update = -4.775 * inner + 2.0315 * squared
            iterate = 3.4445 * iterate + jnp.dot(merged_update, iterate, precision=top_precision)
        new_basis = new_basis.at[group, :, place, :].set(iterate)
    return (jnp.stack(trained), new_basis)
```

```python
import jax
import jax.numpy as jnp
from jax import lax
from jax.experimental import pallas as pl
from jax.experimental.pallas import tpu as pltpu
from jax.sharding import PartitionSpec as P

NS_ITERS = 4
BF = jnp.bfloat16
F32 = jnp.float32


def halves(x):
    hi = x.astype(BF)
    return hi, (x - hi.astype(F32)).astype(BF)


def product(a, b, dims):
    (ah, al), (bh, bl) = a, b

    def dot(p, q):
        return lax.dot_general(p, q, (dims, ((), ())), preferred_element_type=F32)

    return dot(ah, bh) + (dot(ah, bl) + dot(al, bh))


NN = ((1,), (0,))
NT = ((1,), (1,))
TN = ((0,), (0,))


def weights_kernel(chosen_ref, basis_ref, grad_ref, m1_ref, m2_ref, master_ref, out_ref, work_ref):
    basis = halves(basis_ref[0])
    turned = product(basis, halves(grad_ref[0]), TN)
    first = 0.9 * m1_ref[0] + 0.1 * turned
    second = 0.95 * m2_ref[0] + 0.05 * turned * turned
    direction = product(basis, halves(first / (jnp.sqrt(second) + 1e-08)), NN)
    held = master_ref[0]
    groups, block_rows = out_ref.shape[1:3]
    slot = pl.program_id(0)
    if block_rows % 8:
        out_ref[0] = (held - 0.1 * (direction + 0.1 * held)).reshape(out_ref.shape[1:])
        return
    work_ref[...] = held - 0.1 * (direction + 0.1 * held)
    for g in range(groups):
        start = pl.multiple_of(chosen_ref[slot, g] * block_rows, 8)
        out_ref[0, g] = work_ref[pl.ds(start, block_rows), :]


def new_weights(chosen, basis, grad, m1, m2, master):
    slots, d, c = grad.shape
    groups = chosen.shape[1]
    if (d // groups) % 8:
        whole = weights_call(chosen, basis, grad, m1, m2, master, (slots, 1, d, c))
        whole = whole.reshape(slots, groups, d // groups, c)
        pick = lambda s, g: lax.dynamic_index_in_dim(whole[s], chosen[s, g], 0, keepdims=False)
        return jnp.stack([jnp.stack([pick(s, g) for g in range(groups)]) for s in range(slots)])
    return weights_call(chosen, basis, grad, m1, m2, master, (slots, groups, d // groups, c))


def weights_call(chosen, basis, grad, m1, m2, master, out_shape):
    slots, d, c = grad.shape
    wide = pl.BlockSpec((1, d, c), lambda i: (i, 0, 0))
    return pl.pallas_call(
        weights_kernel,
        grid=(slots,),
        out_shape=jax.ShapeDtypeStruct(out_shape, F32),
        in_specs=[
            pl.BlockSpec(memory_space=pltpu.SMEM),
            pl.BlockSpec((1, d, d), lambda i: (i, 0, 0)),
            wide,
            wide,
            wide,
            wide,
        ],
        out_specs=pl.BlockSpec((1,) + out_shape[1:], lambda i: (i, 0, 0, 0)),
        scratch_shapes=[pltpu.VMEM((d, c), F32)],
        cost_estimate=pl.CostEstimate(
            flops=12 * slots * d * d * c, bytes_accessed=4 * slots * (d * d + 5 * d * c), transcendentals=0
        ),
        compiler_params=pltpu.CompilerParams(vmem_limit_bytes=48 * 2**20),
        name="weights",
    )(chosen, basis, grad, m1, m2, master)


def refresh_kernel(grad_ref, factor_ref, basis_ref, out_ref):
    d = basis_ref.shape[0]
    outer = jnp.zeros((d, d), F32)
    for j in range(grad_ref.shape[0]):
        g = halves(grad_ref[j])
        outer = outer + product(g, g, NT)
    statistic = 0.95 * factor_ref[...] + 0.05 * outer
    power = product(halves(statistic), halves(basis_ref[...]), NN)
    out_ref[...] = power / jnp.sqrt(jnp.sum(power * power) + 1e-06)

    @pl.loop(0, NS_ITERS)
    def _(step):
        x = out_ref[...]
        xs = halves(x)
        inner = product(xs, xs, NT)
        ins = halves(inner)
        merged = -4.775 * inner + 2.0315 * product(ins, ins, NN)
        out_ref[...] = 3.4445 * x + product(halves(merged), xs, NN)


def refresh(grad, factor, basis):
    d = basis.shape[0]
    return pl.pallas_call(
        refresh_kernel,
        out_shape=jax.ShapeDtypeStruct((d, d), F32),
        in_specs=[pl.BlockSpec(memory_space=pltpu.VMEM)] * 3,
        out_specs=pl.BlockSpec(memory_space=pltpu.VMEM),
        cost_estimate=pl.CostEstimate(flops=90 * d**3, bytes_accessed=4 * 6 * d * d, transcendentals=0),
        compiler_params=pltpu.CompilerParams(vmem_limit_bytes=56 * 2**20),
        name="refresh",
    )(grad, factor, basis)


def body(partials, owner, rowblock, factor, basis, moment1, moment2, master):
    groups = lax.axis_size("dp")
    parts = lax.axis_size("mp")
    my_index = lax.axis_index("dp")
    mine = lax.axis_index("mp")
    count = owner.shape[0]
    rows, slots, d = factor.shape[1:]
    order = jnp.arange(count)
    same = owner[:, None] == owner[None, :]
    slot = jnp.sum((same & (order[None, :] < order[:, None])).astype(jnp.int32), axis=1)
    hits = (owner[None, :] == my_index) & (slot[None, :] == jnp.arange(slots)[:, None])
    valid = jnp.any(hits, axis=1)
    my_matrix = jnp.sum(hits.astype(jnp.int32) * order[None, :], axis=1)

    basis_all = lax.all_gather(jnp.swapaxes(basis[0], 0, 1), "mp", axis=0)
    factor_all = lax.all_gather(jnp.swapaxes(factor[0], 0, 1), "mp", axis=0)

    summed = lax.psum(partials[0].astype(F32), "dp")
    grad = jnp.stack(
        [
            jnp.where(valid[s], lax.dynamic_index_in_dim(summed, my_matrix[s], 0, keepdims=False), 0.0)
            for s in range(slots)
        ]
    ) * (1.0 / groups)

    whole_basis = jnp.swapaxes(basis_all, 0, 1).reshape(slots, d, d)
    chosen = jnp.stack(
        [lax.dynamic_index_in_dim(rowblock, my_matrix[s], 0, keepdims=False) for s in range(slots)]
    )
    sending = new_weights(chosen, whole_basis, grad, moment1[0], moment2[0], master[0])
    grad_all = lax.all_gather(grad, "mp", axis=0)

    my_slot = mine % slots
    take = lambda a: lax.dynamic_index_in_dim(a, my_slot, 1, keepdims=False)
    iterate = refresh(
        take(grad_all),
        take(factor_all).reshape(d, d),
        lax.dynamic_index_in_dim(whole_basis, my_slot, 0, keepdims=False),
    )
    iterate = jnp.where(valid[my_slot], iterate, 0.0).reshape(parts, rows, d)
    block = lambda i: lax.dynamic_index_in_dim(iterate, i, 0, keepdims=False)
    base = mine - my_slot
    pieces = [block(mine)]
    for off in range(1, slots):
        pairs = [(i, i // slots * slots + (i + off) % slots) for i in range(parts)]
        pieces.append(lax.ppermute(block(base + (my_slot + off) % slots), "mp", pairs))
    stacked = jnp.stack(pieces)
    new_basis = jnp.stack(
        [lax.dynamic_index_in_dim(stacked, (my_slot - s) % slots, 0, keepdims=False) for s in range(slots)], axis=1
    )[None]

    received = lax.all_to_all(sending, "dp", split_axis=1, concat_axis=0, tiled=True)
    place = owner * slots + slot
    train_weights = jnp.stack(
        [lax.dynamic_index_in_dim(received, place[m], 0, keepdims=False) for m in range(count)]
    )
    return (train_weights, new_basis)


def solution(mesh):
    placed = (
        P("dp", None, None, "mp"),
        P(),
        P(),
        P("dp", "mp", None, None),
        P("dp", "mp", None, None),
        P("dp", None, None, "mp"),
        P("dp", None, None, "mp"),
        P("dp", None, None, "mp"),
    )
    return jax.shard_map(
        body,
        mesh=mesh,
        in_specs=placed,
        out_specs=(P(None, "dp", None, "mp"), P("dp", "mp", None, None)),
        check_vma=False,
    )
```

```python
import jax
import jax.numpy as jnp
from jax import lax
from jax.experimental import pallas as pl
from jax.experimental.pallas import tpu as pltpu
from jax.sharding import PartitionSpec as P

NS_ITERS = 4
BF = jnp.bfloat16
F32 = jnp.float32


def halves(x):
    hi = x.astype(BF)
    return hi, (x - hi.astype(F32)).astype(BF)


def product(a, b, dims):
    (ah, al), (bh, bl) = a, b

    def dot(p, q):
        return lax.dot_general(p, q, (dims, ((), ())), preferred_element_type=F32)

    return dot(ah, bh) + (dot(ah, bl) + dot(al, bh))


NN = ((1,), (0,))
NT = ((1,), (1,))
TN = ((0,), (0,))


def weights_kernel(chosen_ref, basis_ref, grad_ref, m1_ref, m2_ref, master_ref, out_ref, work_ref):
    basis = halves(basis_ref[0])
    turned = product(basis, halves(grad_ref[0]), TN)
    first = 0.9 * m1_ref[0] + 0.1 * turned
    second = 0.95 * m2_ref[0] + 0.05 * turned * turned
    direction = product(basis, halves(first / (jnp.sqrt(second) + 1e-08)), NN)
    held = master_ref[0]
    groups, block_rows = out_ref.shape[1:3]
    slot = pl.program_id(0)
    if block_rows % 8:
        out_ref[0] = (held - 0.1 * (direction + 0.1 * held)).reshape(out_ref.shape[1:])
        return
    work_ref[...] = held - 0.1 * (direction + 0.1 * held)
    for g in range(groups):
        start = pl.multiple_of(chosen_ref[slot, g] * block_rows, 8)
        out_ref[0, g] = work_ref[pl.ds(start, block_rows), :]


def new_weights(chosen, basis, grad, m1, m2, master):
    slots, d, c = grad.shape
    groups = chosen.shape[1]
    if (d // groups) % 8:
        whole = weights_call(chosen, basis, grad, m1, m2, master, (slots, 1, d, c))
        whole = whole.reshape(slots, groups, d // groups, c)
        pick = lambda s, g: lax.dynamic_index_in_dim(whole[s], chosen[s, g], 0, keepdims=False)
        return jnp.stack([jnp.stack([pick(s, g) for g in range(groups)]) for s in range(slots)])
    return weights_call(chosen, basis, grad, m1, m2, master, (slots, groups, d // groups, c))


def weights_call(chosen, basis, grad, m1, m2, master, out_shape):
    slots, d, c = grad.shape
    wide = pl.BlockSpec((1, d, c), lambda i: (i, 0, 0))
    return pl.pallas_call(
        weights_kernel,
        grid=(slots,),
        out_shape=jax.ShapeDtypeStruct(out_shape, F32),
        in_specs=[
            pl.BlockSpec(memory_space=pltpu.SMEM),
            pl.BlockSpec((1, d, d), lambda i: (i, 0, 0)),
            wide,
            wide,
            wide,
            wide,
        ],
        out_specs=pl.BlockSpec((1,) + out_shape[1:], lambda i: (i, 0, 0, 0)),
        scratch_shapes=[pltpu.VMEM((d, c), F32)],
        cost_estimate=pl.CostEstimate(
            flops=12 * slots * d * d * c, bytes_accessed=4 * slots * (d * d + 5 * d * c), transcendentals=0
        ),
        compiler_params=pltpu.CompilerParams(vmem_limit_bytes=48 * 2**20),
        name="weights",
    )(chosen, basis, grad, m1, m2, master)


def refresh_kernel(grad_ref, factor_ref, basis_ref, out_ref):
    d = basis_ref.shape[0]
    outer = jnp.zeros((d, d), F32)
    for j in range(grad_ref.shape[0]):
        g = halves(grad_ref[j])
        outer = outer + product(g, g, NT)
    statistic = 0.95 * factor_ref[...] + 0.05 * outer
    power = product(halves(statistic), halves(basis_ref[...]), NN)
    out_ref[...] = power / jnp.sqrt(jnp.sum(power * power) + 1e-06)

    @pl.loop(0, NS_ITERS)
    def _(step):
        x = out_ref[...]
        xs = halves(x)
        inner = product(xs, xs, NT)
        ins = halves(inner)
        merged = -4.775 * inner + 2.0315 * product(ins, ins, NN)
        out_ref[...] = 3.4445 * x + product(halves(merged), xs, NN)


def refresh(grad, factor, basis):
    d = basis.shape[0]
    return pl.pallas_call(
        refresh_kernel,
        out_shape=jax.ShapeDtypeStruct((d, d), F32),
        in_specs=[pl.BlockSpec(memory_space=pltpu.VMEM)] * 3,
        out_specs=pl.BlockSpec(memory_space=pltpu.VMEM),
        cost_estimate=pl.CostEstimate(flops=90 * d**3, bytes_accessed=4 * 6 * d * d, transcendentals=0),
        compiler_params=pltpu.CompilerParams(vmem_limit_bytes=56 * 2**20),
        name="refresh",
    )(grad, factor, basis)


def body(partials, owner, rowblock, factor, basis, moment1, moment2, master):
    groups = lax.axis_size("dp")
    parts = lax.axis_size("mp")
    my_index = lax.axis_index("dp")
    mine = lax.axis_index("mp")
    count = owner.shape[0]
    rows, slots, d = factor.shape[1:]
    order = jnp.arange(count)
    same = owner[:, None] == owner[None, :]
    slot = jnp.sum((same & (order[None, :] < order[:, None])).astype(jnp.int32), axis=1)
    hits = (owner[None, :] == my_index) & (slot[None, :] == jnp.arange(slots)[:, None])
    valid = jnp.any(hits, axis=1)
    my_matrix = jnp.sum(hits.astype(jnp.int32) * order[None, :], axis=1)

    basis_all = lax.all_gather(jnp.swapaxes(basis[0], 0, 1), "mp", axis=0)
    factor_all = lax.all_gather(jnp.swapaxes(factor[0], 0, 1), "mp", axis=0)

    local = partials[0].astype(F32) * (1.0 / groups)
    pick = lambda a, m, ok: jnp.where(ok, lax.dynamic_index_in_dim(a, m, 0, keepdims=False), 0.0)

    def whole_sum():
        summed = lax.psum(local, "dp")
        return jnp.stack([pick(summed, my_matrix[s], valid[s]) for s in range(slots)])

    def owners_sum():
        units = []
        for g in range(groups):
            hit = (owner == g) & (slot == 0)
            units.append(pick(local, jnp.sum(hit * order), jnp.any(hit)))
        lead = lax.psum_scatter(jnp.stack(units), "dp", scatter_dimension=0)
        second = lax.psum(pick(local, jnp.sum((slot == 1) * order), jnp.any(slot == 1)), "dp")
        return jnp.stack([lead, jnp.where(valid[1], second, 0.0)])

    if groups <= count and slots == 2:
        grad = lax.cond(jnp.sum(slot == 1) <= 1, owners_sum, whole_sum)
    else:
        grad = whole_sum()

    whole_basis = jnp.swapaxes(basis_all, 0, 1).reshape(slots, d, d)
    chosen = jnp.stack(
        [lax.dynamic_index_in_dim(rowblock, my_matrix[s], 0, keepdims=False) for s in range(slots)]
    )
    sending = new_weights(chosen, whole_basis, grad, moment1[0], moment2[0], master[0])
    grad_all = lax.all_gather(grad, "mp", axis=0)

    my_slot = mine % slots
    take = lambda a: lax.dynamic_index_in_dim(a, my_slot, 1, keepdims=False)
    iterate = refresh(
        take(grad_all),
        take(factor_all).reshape(d, d),
        lax.dynamic_index_in_dim(whole_basis, my_slot, 0, keepdims=False),
    )
    iterate = jnp.where(valid[my_slot], iterate, 0.0).reshape(parts, rows, d)
    block = lambda i: lax.dynamic_index_in_dim(iterate, i, 0, keepdims=False)
    base = mine - my_slot
    pieces = [block(mine)]
    for off in range(1, slots):
        pairs = [(i, i // slots * slots + (i + off) % slots) for i in range(parts)]
        pieces.append(lax.ppermute(block(base + (my_slot + off) % slots), "mp", pairs))
    stacked = jnp.stack(pieces)
    new_basis = jnp.stack(
        [lax.dynamic_index_in_dim(stacked, (my_slot - s) % slots, 0, keepdims=False) for s in range(slots)], axis=1
    )[None]

    received = lax.all_to_all(sending, "dp", split_axis=1, concat_axis=0, tiled=True)
    place = owner * slots + slot
    train_weights = jnp.stack(
        [lax.dynamic_index_in_dim(received, place[m], 0, keepdims=False) for m in range(count)]
    )
    return (train_weights, new_basis)


def solution(mesh):
    placed = (
        P("dp", None, None, "mp"),
        P(),
        P(),
        P("dp", "mp", None, None),
        P("dp", "mp", None, None),
        P("dp", None, None, "mp"),
        P("dp", None, None, "mp"),
        P("dp", None, None, "mp"),
    )
    return jax.shard_map(
        body,
        mesh=mesh,
        in_specs=placed,
        out_specs=(P(None, "dp", None, "mp"), P("dp", "mp", None, None)),
        check_vma=False,
    )
```
